32 devices in a mesh: rows: 8 (over z, x), cols: 4 (over y, core).
Axes of the slice: x: 2, y: 2, z: 4, core: 2. Of those that a mesh axis runs over, the one named last changes fastest.
Arguments:
- capsule_points: float32 [3, 16384], P(None, 'rows'), may hold values from 0 to 1
- capsule_weight: float32 [16384], P('rows'), may hold values from 0.3 to 9
- wall_points: float32 [3, 8192], P(None, 'cols'), may hold values from 0 to 1
- wall_weight: float32 [8192], P('cols'), may hold values from 0.3 to 3
- gauss_sketch: bfloat16 [8192, 512], P('cols'), may hold values from -0.0625 to 0.0625
- far_pairs: int32 [8, 4, 48, 2], P('rows', 'cols'), may hold values from -1 to 63, as said below
- tile_count: int32 [8, 4], P('rows', 'cols'), may hold values from 16 to 48, as said below
Outputs:
- basis_out: bfloat16 [16384, 512], P(('rows', 'cols'))
- projected: float32 [512, 8192], P('rows', 'cols')
The draws below stay inside these ranges and needn't reach their ends.
Inputs may be any that keep to these rules, and one draw needn't show every extreme that they name: For every p and q the first tile_count[p, q] entries of far_pairs[p, q] are distinct pairs whose row block lies in p * 8 to (p + 1) * 8 - 1 and whose column block lies in q * 8 to (q + 1) * 8 - 1; the later entries are -1 and name no tile. `tile_count`: some device has exactly 48 far tiles in every draw.
All inputs are finite; a program needn't handle non-finite values.
Results may differ from the reference program's by a relative error of at most 0.0052.
Values may be sent and summed in bfloat16 or wider, within the bound.
A program may use at most 128 MiB of HBM per device.

```python
import math
import jax
import jax.numpy as jnp
from jax import lax

TILE = 256
SAMPLES = 512
ROW_BLOCKS = 8
COL_BLOCKS = 8
MAX_TILES = 48
CAPSULE_PTS = 16384
WALL_PTS = 8192
N_ROWS = 8
N_COLS = 4


def pattern_tables(key):
    devices_all = N_ROWS * N_COLS
    slots_all = ROW_BLOCKS * COL_BLOCKS
    least_tiles = max(1, MAX_TILES // 3)
    heavy_rows = jax.random.randint(jax.random.fold_in(key, 11), (devices_all,), 0, 8) == 0
    big_extra = jax.random.randint(jax.random.fold_in(key, 12), (devices_all,), 0, MAX_TILES - least_tiles + 1)
    small_extra = jax.random.randint(jax.random.fold_in(key, 13), (devices_all,), 0, (MAX_TILES - least_tiles) // 4 + 1)
    counts = least_tiles + jnp.where(heavy_rows, big_extra, small_extra)
    chosen = jax.random.randint(jax.random.fold_in(key, 14), (), 0, devices_all)
    device_ids = jnp.arange(devices_all, dtype=jnp.int32)
    counts = jnp.where(device_ids == chosen, MAX_TILES, counts).astype(jnp.int32)
    perm_keys = jax.random.split(jax.random.fold_in(key, 15), devices_all)
    full_orders = jax.vmap(lambda subkey: jax.random.permutation(subkey, slots_all))(perm_keys)
    top_slot = slots_all - 1
    first_slot = full_orders[:, 0]
    swapped = jnp.where(full_orders == top_slot, first_slot[:, None], full_orders)
    swapped = swapped.at[:, 0].set(top_slot)
    last_device = (device_ids == devices_all - 1)[:, None]
    orders = jnp.where(last_device, swapped, full_orders)[:, :MAX_TILES]
    row_dev = device_ids // N_COLS
    col_dev = device_ids % N_COLS
    rows_global = row_dev[:, None] * ROW_BLOCKS + orders // COL_BLOCKS
    cols_global = col_dev[:, None] * COL_BLOCKS + orders % COL_BLOCKS
    live_slot = jnp.arange(MAX_TILES, dtype=jnp.int32)[None, :] < counts[:, None]
    rows_global = jnp.where(live_slot, rows_global, -1)
    cols_global = jnp.where(live_slot, cols_global, -1)
    tile_pairs = jnp.stack([rows_global, cols_global], axis=-1).reshape(N_ROWS, N_COLS, MAX_TILES, 2).astype(jnp.int32)
    return (tile_pairs, counts.reshape(N_ROWS, N_COLS))


def draw_far_pairs(key, part):
    return pattern_tables(key)[0]


def draw_tile_count(key, part):
    return pattern_tables(key)[1]


def draw_capsule_weight(key, part):
    rising = 1.0 + 2.0 * jnp.arange(CAPSULE_PTS, dtype=jnp.float32) / CAPSULE_PTS
    spread = jnp.exp(jax.random.uniform(key, (CAPSULE_PTS,), jnp.float32, jnp.log(0.3), jnp.log(3.0)))
    return spread * rising


def shard_levels(own_key, dims, cuts, low, top_value):
    def one(dim, shards_of):
        heights = jax.random.uniform(jax.random.fold_in(jax.random.fold_in(own_key, 6), dim), (shards_of,), jnp.float32, low / len(cuts), top_value / len(cuts))
        return jnp.repeat(jnp.exp(heights), dims[dim] // shards_of).reshape((-1,) + (1,) * (len(dims) - dim - 1))

    level = one(*cuts[0])
    for cut in cuts[1:]:
        level = level * one(*cut)
    return level


def scatter_about(own_key, shape, scale, reach, cuts=(), kind=jnp.bfloat16):
    factor_of = shard_levels(own_key, shape, cuts, -0.22, 0.18) if cuts else 1.0
    array = jax.random.normal(own_key, shape, jnp.float32) * scale * factor_of
    return jnp.minimum(jnp.maximum(array, -reach), reach).astype(kind)


def setup_inputs(seed: int = 0) -> dict:
    seeds = jax.random.split(jax.random.key(seed), 8)
    return {
        "capsule_points": jnp.clip(1.0 * jax.random.uniform(seeds[0], (3, CAPSULE_PTS), jnp.float32) ** shard_levels(seeds[0], (3, CAPSULE_PTS), ((1, 8),), -0.2, 0.2), 0.0, 1.0),
        "capsule_weight": draw_capsule_weight(jax.random.fold_in(seeds[7], 71), 0),
        "wall_points": jnp.clip(1.0 * jax.random.uniform(seeds[2], (3, WALL_PTS), jnp.float32) ** shard_levels(seeds[2], (3, WALL_PTS), ((1, 4),), -0.2, 0.2), 0.0, 1.0),
        "wall_weight": jnp.clip(jnp.exp(math.log(3.0) - 2.3025851 * jax.random.uniform(seeds[3], (WALL_PTS,), jnp.float32) ** shard_levels(seeds[3], (WALL_PTS,), ((0, 4),), -0.2, 0.2)), 0.3, 3.0),
        "gauss_sketch": scatter_about(seeds[4], (WALL_PTS, SAMPLES), WALL_PTS ** -0.5, 0.0625, ((0, 4),)),
        "far_pairs": draw_far_pairs(jax.random.fold_in(seeds[7], 71), 0),
        "tile_count": draw_tile_count(jax.random.fold_in(seeds[7], 71), 0),
    }


WAVENUMBER = 150.0
WALL_GAP = 2.0

def kernel_tiles(row_points, row_weight, col_points, col_weight):
    diff_x = row_points[:, 0, :, None] - col_points[:, 0, None, :]
    diff_y = row_points[:, 1, :, None] - col_points[:, 1, None, :]
    diff_z = row_points[:, 2, :, None] - col_points[:, 2, None, :] - WALL_GAP
    distance = jnp.sqrt(diff_x * diff_x + diff_y * diff_y + diff_z * diff_z)
    return (row_weight[:, :, None] * col_weight[:, None, :] * jnp.cos(WAVENUMBER * distance) / distance).astype(jnp.bfloat16)

def reference(capsule_points, capsule_weight, wall_points, wall_weight, gauss_sketch, far_pairs, tile_count):
    row_total = N_ROWS * ROW_BLOCKS
    col_total = N_COLS * COL_BLOCKS
    capsule_blocks = jnp.transpose(capsule_points.reshape(3, row_total, TILE), (1, 0, 2))
    capsule_wblocks = capsule_weight.reshape(row_total, TILE)
    wall_blocks = jnp.transpose(wall_points.reshape(3, col_total, TILE), (1, 0, 2))
    wall_wblocks = wall_weight.reshape(col_total, TILE)
    sketch_blocks = gauss_sketch.reshape(col_total, TILE, SAMPLES)
    live_slots = jnp.arange(MAX_TILES, dtype=jnp.int32)[None, None, :] < tile_count[:, :, None]

    def device_tiles(row_dev):
        live_here = live_slots[row_dev].reshape(-1)
        pair_rows = jnp.where(live_here, far_pairs[row_dev, :, :, 0].reshape(-1), row_dev * ROW_BLOCKS).astype(jnp.int32)
        pair_cols = jnp.where(live_here, far_pairs[row_dev, :, :, 1].reshape(-1), 0).astype(jnp.int32)
        tiles = kernel_tiles(capsule_blocks[pair_rows], capsule_wblocks[pair_rows], wall_blocks[pair_cols], wall_wblocks[pair_cols])
        tiles = jnp.where(live_here[:, None, None], tiles, jnp.zeros_like(tiles))
        return (tiles, pair_rows, pair_cols)

    def sketch_rows(row_dev):
        tiles, pair_rows, pair_cols = device_tiles(row_dev)
        products = jnp.einsum('tij,tjk->tik', tiles.astype(jnp.float32), sketch_blocks[pair_cols].astype(jnp.float32))
        local_rows = (pair_rows - row_dev * ROW_BLOCKS).astype(jnp.int32)
        onehot = (local_rows[:, None] == jnp.arange(ROW_BLOCKS, dtype=jnp.int32)[None, :]).astype(jnp.float32)
        return jnp.einsum('tb,tik->bik', onehot, products).reshape(ROW_BLOCKS * TILE, SAMPLES)
    sketch_y = lax.map(sketch_rows, jnp.arange(N_ROWS, dtype=jnp.int32)).reshape(CAPSULE_PTS, SAMPLES)
    gram = jnp.dot(sketch_y.T.astype(jnp.float32), sketch_y.astype(jnp.float32), precision=lax.Precision.HIGHEST, preferred_element_type=jnp.float32)
    lower = jnp.linalg.cholesky(gram)
    inverse = jax.scipy.linalg.solve_triangular(lower, jnp.eye(SAMPLES, dtype=jnp.float32), lower=True)
    q_float = jnp.dot(sketch_y.astype(jnp.float32), inverse.T.astype(jnp.float32), precision=lax.Precision.HIGHEST, preferred_element_type=jnp.float32)
    basis_out = (math.sqrt(CAPSULE_PTS) * q_float).astype(jnp.bfloat16)
    q_round = q_float.astype(jnp.bfloat16)
    basis_blocks = q_round.reshape(row_total, TILE, SAMPLES)

    def project_rows(running, row_dev):
        tiles, pair_rows, pair_cols = device_tiles(row_dev)
        contrib = jnp.einsum('tik,tij->tkj', basis_blocks[pair_rows].astype(jnp.float32), tiles.astype(jnp.float32))
        onehot = (pair_cols[:, None] == jnp.arange(col_total, dtype=jnp.int32)[None, :]).astype(jnp.float32)
        placed = jnp.einsum('tc,tkj->kcj', onehot, contrib).reshape(SAMPLES, WALL_PTS)
        return (running + placed, None)
    projected, unused = lax.scan(project_rows, jnp.zeros((SAMPLES, WALL_PTS), jnp.float32), jnp.arange(N_ROWS, dtype=jnp.int32))
    return (basis_out, projected)
```

```python
import functools
import math

import jax
import jax.numpy as jnp
import numpy as np
from jax import lax
from jax.experimental import pallas as pl
from jax.experimental.pallas import tpu as pltpu
from jax.sharding import PartitionSpec as P

TILE = 256


WAVENUMBER = 150.0
WALL_GAP = 2.0
HIGHEST = lax.Precision.HIGHEST
CHUNK = 32
TURN_HIGH = 6.28125
TURN_LOW = float(2.0 * np.pi - 6.28125)


def half_cos_terms(degree=4):
    top = np.pi**2 * 1.0001
    series = np.polynomial.Chebyshev.interpolate(
        lambda w: np.cos(np.sqrt(np.maximum(w, 0.0)) / 2.0), degree, domain=[0.0, top]
    )
    return [float(c) for c in series.convert(kind=np.polynomial.Polynomial).coef]


def tile_values(row_part, col_part):
    diff_x = row_part[:, 0:1] - col_part[0:1, :]
    diff_y = row_part[:, 1:2] - col_part[1:2, :]
    diff_z = row_part[:, 2:3] - col_part[2:3, :] - WALL_GAP
    square = diff_x * diff_x + diff_y * diff_y + diff_z * diff_z
    inverse = lax.rsqrt(square)
    distance = square * inverse
    distance = distance + (0.5 * inverse) * (square - distance * distance)
    angle = WAVENUMBER * distance
    turns = jnp.floor(angle * float(0.5 / np.pi) + 0.5)
    rest = (angle - turns * TURN_HIGH) - turns * TURN_LOW
    w = rest * rest
    terms = half_cos_terms()
    half = jnp.full_like(w, terms[-1])
    for term in terms[-2::-1]:
        half = half * w + term
    cosine = 2.0 * (half * half) - 1.0
    return (row_part[:, 3:4] * col_part[3:4, :]) * cosine * inverse


def tiles_kernel(list_ref, count_ref, rows_ref, walls_ref, matrix_ref):
    tile = walls_ref.shape[2]
    matrix_ref[...] = jnp.zeros_like(matrix_ref)

    def slot(index, carry):
        row_block = list_ref[index, 0]
        col_block = list_ref[index, 1]
        col_part = walls_ref[col_block]

        def chunk(step, inner):
            start = pl.multiple_of(row_block * tile + step * CHUNK, CHUNK)
            values = tile_values(rows_ref[pl.ds(start, CHUNK), :], col_part)
            matrix_ref[col_block, pl.ds(start, CHUNK), :] = values.astype(jnp.bfloat16)
            return inner

        return lax.fori_loop(0, tile // CHUNK, chunk, carry, unroll=2)

    lax.fori_loop(0, count_ref[0], slot, 0)


def dense_tiles(capsule_points, capsule_weight, wall_points, wall_weight, local_list, count):
    local_rows = capsule_points.shape[1]
    col_blocks = wall_points.shape[1] // TILE
    rows = jnp.concatenate([capsule_points, capsule_weight[None]], axis=0).T
    walls = jnp.concatenate([wall_points, wall_weight[None]], axis=0)
    walls = walls.reshape(4, col_blocks, TILE).transpose(1, 0, 2)
    smem = pl.BlockSpec(memory_space=pltpu.SMEM)
    vmem = pl.BlockSpec(memory_space=pltpu.VMEM)
    return pl.pallas_call(
        tiles_kernel,
        out_shape=jax.ShapeDtypeStruct((col_blocks, local_rows, TILE), jnp.bfloat16),
        in_specs=[smem, smem, vmem, vmem],
        out_specs=vmem,
        compiler_params=pltpu.CompilerParams(vmem_limit_bytes=40 * 2**20),
    )(local_list, count, rows, walls)


def basis_map(gram_total, identity):
    lower = jnp.linalg.cholesky(gram_total)
    inverse = jax.scipy.linalg.solve_triangular(lower, identity, lower=True)
    return inverse.T


def per_device(
    capsule_points, capsule_weight, wall_points, wall_weight, gauss_sketch, far_pairs, tile_count
):
    row_dev = lax.axis_index("rows")
    col_dev = lax.axis_index("cols")
    local_rows = capsule_points.shape[1]
    wall_cells = wall_points.shape[1]
    row_blocks = local_rows // TILE
    col_blocks = wall_cells // TILE
    samples = gauss_sketch.shape[1]
    offset = jnp.stack([row_dev * row_blocks, col_dev * col_blocks]).astype(jnp.int32)
    matrix = dense_tiles(
        capsule_points,
        capsule_weight,
        wall_points,
        wall_weight,
        far_pairs[0, 0] - offset[None, :],
        tile_count[0],
    )
    partial_y = lax.dot_general(
        matrix,
        gauss_sketch.reshape(col_blocks, TILE, samples),
        (((0, 2), (0, 1)), ((), ())),
        preferred_element_type=jnp.float32,
    )
    basis_scale = math.sqrt(local_rows * lax.axis_size("rows"))
    share_y = lax.psum_scatter(partial_y, "cols", scatter_dimension=0, tiled=True)
    gram = lax.dot_general(
        share_y,
        share_y,
        (((0,), (0,)), ((), ())),
        precision=HIGHEST,
        preferred_element_type=jnp.float32,
    )
    gram_total = lax.psum(gram, ("rows", "cols"))
    share_q = jnp.dot(
        share_y,
        basis_map(gram_total, jnp.eye(samples, dtype=jnp.float32)),
        precision=HIGHEST,
        preferred_element_type=jnp.float32,
    )
    basis_out = (basis_scale * share_q).astype(jnp.bfloat16)
    q_round = lax.all_gather(share_q.astype(jnp.bfloat16), "cols", axis=0, tiled=True)
    partial_p = lax.dot_general(
        q_round, matrix, (((0,), (1,)), ((), ())), preferred_element_type=jnp.float32
    ).reshape(samples, wall_cells)
    projected = lax.psum_scatter(partial_p, "rows", scatter_dimension=0, tiled=True)
    return (basis_out, projected)


def solution(mesh):
    placed = (
        P(None, "rows"),
        P("rows"),
        P(None, "cols"),
        P("cols"),
        P("cols", None),
        P("rows", "cols", None, None),
        P("rows", "cols"),
    )
    return jax.shard_map(
        per_device,
        mesh=mesh,
        in_specs=placed,
        out_specs=(P(("rows", "cols"), None), P("rows", "cols")),
        check_vma=False,
    )
```

```python
import functools
import math

import jax
import jax.numpy as jnp
import numpy as np
from jax import lax
from jax.experimental import pallas as pl
from jax.experimental.pallas import tpu as pltpu
from jax.sharding import PartitionSpec as P

TILE = 256


WAVENUMBER = 150.0
WALL_GAP = 2.0
HIGHEST = lax.Precision.HIGHEST
CHUNK = 32
TURN_HIGH = 6.28125
TURN_LOW = float(2.0 * np.pi - 6.28125)


def half_cos_terms(degree=4):
    top = np.pi**2 * 1.0001
    series = np.polynomial.Chebyshev.interpolate(
        lambda w: np.cos(np.sqrt(np.maximum(w, 0.0)) / 2.0), degree, domain=[0.0, top]
    )
    return [float(c) for c in series.convert(kind=np.polynomial.Polynomial).coef]


def tile_values(row_part, col_part):
    diff_x = row_part[:, 0:1] - col_part[0:1, :]
    diff_y = row_part[:, 1:2] - col_part[1:2, :]
    diff_z = row_part[:, 2:3] - col_part[2:3, :] - WALL_GAP
    square = diff_x * diff_x + diff_y * diff_y + diff_z * diff_z
    inverse = lax.rsqrt(square)
    distance = square * inverse
    distance = distance + (0.5 * inverse) * (square - distance * distance)
    angle = WAVENUMBER * distance
    turns = jnp.floor(angle * float(0.5 / np.pi) + 0.5)
    rest = (angle - turns * TURN_HIGH) - turns * TURN_LOW
    w = rest * rest
    terms = half_cos_terms()
    half = jnp.full_like(w, terms[-1])
    for term in terms[-2::-1]:
        half = half * w + term
    cosine = 2.0 * (half * half) - 1.0
    return (row_part[:, 3:4] * col_part[3:4, :]) * cosine * inverse


def tiles_kernel(list_ref, count_ref, rows_ref, walls_ref, matrix_ref):
    tile = walls_ref.shape[2]
    matrix_ref[...] = jnp.zeros_like(matrix_ref)

    def slot(index, carry):
        row_block = list_ref[index, 0]
        col_block = list_ref[index, 1]
        col_part = walls_ref[col_block]

        def chunk(step, inner):
            start = pl.multiple_of(row_block * tile + step * CHUNK, CHUNK)
            values = tile_values(rows_ref[pl.ds(start, CHUNK), :], col_part)
            matrix_ref[col_block, pl.ds(start, CHUNK), :] = values.astype(jnp.bfloat16)
            return inner

        return lax.fori_loop(0, tile // CHUNK, chunk, carry, unroll=2)

    lax.fori_loop(0, count_ref[0], slot, 0)


def dense_tiles(capsule_points, capsule_weight, wall_points, wall_weight, local_list, count):
    local_rows = capsule_points.shape[1]
    col_blocks = wall_points.shape[1] // TILE
    rows = jnp.concatenate([capsule_points, capsule_weight[None]], axis=0).T
    walls = jnp.concatenate([wall_points, wall_weight[None]], axis=0)
    walls = walls.reshape(4, col_blocks, TILE).transpose(1, 0, 2)
    smem = pl.BlockSpec(memory_space=pltpu.SMEM)
    vmem = pl.BlockSpec(memory_space=pltpu.VMEM)
    return pl.pallas_call(
        tiles_kernel,
        out_shape=jax.ShapeDtypeStruct((col_blocks, local_rows, TILE), jnp.bfloat16),
        in_specs=[smem, smem, vmem, vmem],
        out_specs=vmem,
        compiler_params=pltpu.CompilerParams(vmem_limit_bytes=40 * 2**20),
    )(local_list, count, rows, walls)


PANEL = 8
BLOCK = 128


def full_dot(left, right, left_dim, right_dim):
    return lax.dot_general(
        left,
        right,
        (((left_dim,), (right_dim,)), ((), ())),
        precision=HIGHEST,
        preferred_element_type=jnp.float32,
    )


def eliminate_panel(panel, first):
    lanes = lax.broadcasted_iota(jnp.int32, (PANEL, BLOCK), 1)
    subs = lax.broadcasted_iota(jnp.int32, (PANEL, BLOCK), 0)
    left = panel[:, :BLOCK]
    right = panel[:, BLOCK:]
    columns = [
        jnp.broadcast_to(
            jnp.sum(jnp.where(lanes == first + j, left, 0.0), axis=1, keepdims=True),
            (PANEL, BLOCK),
        )
        for j in range(PANEL)
    ]
    for j in range(PANEL):
        pivot = jnp.broadcast_to(columns[j][j : j + 1, :], (PANEL, BLOCK))
        scale = lax.rsqrt(pivot)
        scale = scale * (1.5 - 0.5 * pivot * (scale * scale))
        multiplier = columns[j] * scale

        def step(value):
            row = jnp.broadcast_to(value[j : j + 1, :], (PANEL, BLOCK)) * scale
            return jnp.where(subs == j, row, jnp.where(subs > j, value - multiplier * row, value))

        left = step(left)
        right = step(right)
        for k in range(j + 1, PANEL):
            columns[k] = step(columns[k])
    return left, right


def inverse_kernel(gram_ref, inverse_ref, work, small):
    size = gram_ref.shape[0]
    lanes = lax.broadcasted_iota(jnp.int32, (PANEL, BLOCK), 1)
    rows_eye = lax.broadcasted_iota(jnp.int32, (BLOCK, BLOCK), 0)
    cols_eye = lax.broadcasted_iota(jnp.int32, (BLOCK, BLOCK), 1)
    eye = jnp.where(rows_eye == cols_eye, 1.0, 0.0).astype(jnp.float32)
    work[:, :size] = gram_ref[...]
    work[:, size:] = jnp.zeros((size, size), jnp.float32)
    inverse_ref[...] = jnp.zeros_like(inverse_ref)
    for start in range(0, size, BLOCK):
        stop = start + BLOCK
        small[:, :BLOCK] = work[start:stop, start:stop]
        small[:, BLOCK:] = eye

        def group(index, carry):
            first = pl.multiple_of(index * PANEL, PANEL)
            left, right = eliminate_panel(small[pl.ds(first, PANEL), :], first)
            both = jnp.concatenate([left, right], axis=1)
            below = jnp.where(lanes >= first + PANEL, left, 0.0)
            small[...] = small[...] - full_dot(below, both, 0, 0)
            small[pl.ds(first, PANEL), :] = both
            return carry

        lax.fori_loop(0, BLOCK // PANEL, group, 0)
        block_inverse = small[:, BLOCK:]
        if start:
            known = full_dot(block_inverse, work[start:stop, size : size + start], 1, 0)
            inverse_ref[start:stop, :start] = known
        inverse_ref[start:stop, start:stop] = block_inverse
        if stop < size:
            ahead = full_dot(block_inverse, work[start:stop, stop:size], 1, 0)
            done = inverse_ref[start:stop, :stop]
            work[stop:, stop:size] = work[stop:, stop:size] - full_dot(ahead, ahead, 0, 0)
            work[stop:, size : size + stop] = work[stop:, size : size + stop] - full_dot(
                ahead, done, 0, 0
            )


def lower_inverse(gram_total):
    size = gram_total.shape[0]
    vmem = pl.BlockSpec(memory_space=pltpu.VMEM)
    return pl.pallas_call(
        inverse_kernel,
        out_shape=jax.ShapeDtypeStruct((size, size), jnp.float32),
        in_specs=[vmem],
        out_specs=vmem,
        scratch_shapes=[
            pltpu.VMEM((size, 2 * size), jnp.float32),
            pltpu.VMEM((BLOCK, 2 * BLOCK), jnp.float32),
        ],
        compiler_params=pltpu.CompilerParams(vmem_limit_bytes=32 * 2**20),
    )(gram_total)


def greet(peers):
    barrier = pltpu.get_barrier_semaphore()
    for peer in peers:
        pl.semaphore_signal(
            barrier, inc=1, device_id=peer, device_id_type=pl.DeviceIdType.MESH
        )
    pl.semaphore_wait(barrier, len(peers))


def send(source, target, send_sem, recv_sem, peer):
    copy = pltpu.make_async_remote_copy(
        src_ref=source,
        dst_ref=target,
        send_sem=send_sem,
        recv_sem=recv_sem,
        device_id=peer,
        device_id_type=pl.DeviceIdType.MESH,
    )
    copy.start()
    return copy


def wait_all(copies):
    for copy in copies:
        copy.wait()


def sketch_kernel(
    n_rows,
    n_cols,
    y_ref,
    share_ref,
    gram_ref,
    totals,
    first_in,
    later_out,
    later_in,
    gram_own,
    col_in,
    row_sum,
    row_in,
    whole,
    first_send,
    first_recv,
    later_send,
    later_recv,
    col_send,
    col_recv,
    row_send,
    row_recv,
):
    me_row = lax.axis_index("rows")
    me_col = lax.axis_index("cols")
    row_peers = [
        (lax.rem(me_row + d, n_rows), me_col) for d in range(1, n_rows)
    ]
    col_peers = [
        (me_row, lax.rem(me_col + d, n_cols)) for d in range(1, n_cols)
    ]
    greet(row_peers + col_peers)

    half = n_cols // 2
    bit = me_col % 2
    other = (me_row, me_col + 1 - 2 * bit)
    copies = [
        send(y_ref.at[1 - bit + 2 * j], first_in.at[j], first_send.at[j], first_recv.at[j], other)
        for j in range(half)
    ]
    for j in range(half):
        copies[j].wait()
        totals[j] = y_ref[bit + 2 * j] + first_in[j]
    stride, slot = 1, 0
    while stride < half:
        low = (me_col // 2) % stride
        bit = (me_col // (2 * stride)) % 2
        other = (me_row, me_col + 2 * stride * (1 - 2 * bit))
        copies = []
        base = slot
        for j in range(half // (2 * stride)):
            source = low + stride * (1 - bit) + 2 * stride * j
            later_out[slot] = totals[source].astype(jnp.bfloat16)
            copies.append(
                send(
                    later_out.at[slot],
                    later_in.at[slot],
                    later_send.at[slot],
                    later_recv.at[slot],
                    other,
                )
            )
            slot += 1
        for j, copy in enumerate(copies):
            copy.wait()
            kept = low + stride * bit + 2 * stride * j
            totals[kept] = totals[kept] + later_in[base + j].astype(jnp.float32)
        stride *= 2
    share = totals[me_col // 2]
    share_ref[...] = share

    gram = full_dot(share, share, 0, 0)
    gram_own[...] = gram.reshape(gram_own.shape)
    copies = [
        send(gram_own.at[peer[1]], col_in.at[d], col_send.at[0, d], col_recv.at[0, d], peer)
        for d, peer in enumerate(col_peers)
    ]
    wait_all(copies)
    total = gram_own[me_col]
    for d in range(n_cols - 1):
        total = total + col_in[d]
    row_sum[...] = total
    copies = [
        send(row_sum.at[peer[0]], row_in.at[d], row_send.at[0, d], row_recv.at[0, d], peer)
        for d, peer in enumerate(row_peers)
    ]
    wait_all(copies)
    total = row_sum[me_row]
    for d in range(n_rows - 1):
        total = total + row_in[d]
    whole[me_col, me_row] = total
    mine = whole.at[me_col, me_row]
    copies = [
        send(mine, mine, row_send.at[1, d], row_recv.at[1, d], peer)
        for d, peer in enumerate(row_peers)
    ]
    wait_all(copies)
    mine = whole.at[me_col]
    copies = [
        send(mine, mine, col_send.at[1, d], col_recv.at[1, d], peer)
        for d, peer in enumerate(col_peers)
    ]
    wait_all(copies)
    gram_ref[...] = whole[...]


def sketch_and_gram(partial_y):
    n_rows, n_cols = lax.axis_size("rows"), lax.axis_size("cols")
    local_rows, samples = partial_y.shape
    share = local_rows // n_cols
    half = n_cols // 2
    part = samples // (n_rows * n_cols)
    vmem = pl.BlockSpec(memory_space=pltpu.VMEM)
    later = max(half - 1, 1)
    dma = pltpu.SemaphoreType.DMA
    share_y, gram = pl.pallas_call(
        functools.partial(sketch_kernel, n_rows, n_cols),
        out_shape=(
            jax.ShapeDtypeStruct((share, samples), jnp.float32),
            jax.ShapeDtypeStruct((n_cols, n_rows, part, samples), jnp.float32),
        ),
        in_specs=[vmem],
        out_specs=(vmem, vmem),
        scratch_shapes=[
            pltpu.VMEM((half, share, samples), jnp.float32),
            pltpu.VMEM((half, share, samples), jnp.float32),
            pltpu.VMEM((later, share, samples), jnp.bfloat16),
            pltpu.VMEM((later, share, samples), jnp.bfloat16),
            pltpu.VMEM((n_cols, n_rows, part, samples), jnp.float32),
            pltpu.VMEM((n_cols - 1, n_rows, part, samples), jnp.float32),
            pltpu.VMEM((n_rows, part, samples), jnp.float32),
            pltpu.VMEM((n_rows - 1, part, samples), jnp.float32),
            pltpu.VMEM((n_cols, n_rows, part, samples), jnp.float32),
            dma((half,)),
            dma((half,)),
            dma((later,)),
            dma((later,)),
            dma((2, n_cols - 1)),
            dma((2, n_cols - 1)),
            dma((2, n_rows - 1)),
            dma((2, n_rows - 1)),
        ],
        compiler_params=pltpu.CompilerParams(
            collective_id=0, has_side_effects=True, vmem_limit_bytes=48 * 2**20
        ),
    )(partial_y.reshape(n_cols, share, samples))
    return share_y, gram.reshape(samples, samples)


def project_kernel(n_rows, p_ref, out_ref, arrived, send_sem, recv_sem):
    me_row = lax.axis_index("rows")
    me_col = lax.axis_index("cols")
    peers = [(lax.rem(me_row + d, n_rows), me_col) for d in range(1, n_rows)]
    greet(peers)
    copies = [
        send(p_ref.at[peer[0]], arrived.at[d], send_sem.at[d], recv_sem.at[d], peer)
        for d, peer in enumerate(peers)
    ]
    out_ref[...] = p_ref[me_row].astype(jnp.float32)
    for d, copy in enumerate(copies):
        copy.wait()
        out_ref[...] += arrived[d].astype(jnp.float32)


def project_scatter(partial_p):
    n_rows = lax.axis_size("rows")
    samples, wall_cells = partial_p.shape
    part = samples // n_rows
    vmem = pl.BlockSpec(memory_space=pltpu.VMEM)
    return pl.pallas_call(
        functools.partial(project_kernel, n_rows),
        out_shape=jax.ShapeDtypeStruct((part, wall_cells), jnp.float32),
        in_specs=[vmem],
        out_specs=vmem,
        scratch_shapes=[
            pltpu.VMEM((n_rows - 1, part, wall_cells), jnp.bfloat16),
            pltpu.SemaphoreType.DMA((n_rows - 1,)),
            pltpu.SemaphoreType.DMA((n_rows - 1,)),
        ],
        compiler_params=pltpu.CompilerParams(
            collective_id=1, has_side_effects=True, vmem_limit_bytes=32 * 2**20
        ),
    )(partial_p.reshape(n_rows, part, wall_cells))


def per_device(
    capsule_points, capsule_weight, wall_points, wall_weight, gauss_sketch, far_pairs, tile_count
):
    row_dev = lax.axis_index("rows")
    col_dev = lax.axis_index("cols")
    local_rows = capsule_points.shape[1]
    wall_cells = wall_points.shape[1]
    row_blocks = local_rows // TILE
    col_blocks = wall_cells // TILE
    samples = gauss_sketch.shape[1]
    offset = jnp.stack([row_dev * row_blocks, col_dev * col_blocks]).astype(jnp.int32)
    matrix = dense_tiles(
        capsule_points,
        capsule_weight,
        wall_points,
        wall_weight,
        far_pairs[0, 0] - offset[None, :],
        tile_count[0],
    )
    partial_y = lax.dot_general(
        matrix,
        gauss_sketch.reshape(col_blocks, TILE, samples),
        (((0, 2), (0, 1)), ((), ())),
        preferred_element_type=jnp.float32,
    )
    basis_scale = math.sqrt(local_rows * lax.axis_size("rows"))
    share_y, gram_total = sketch_and_gram(partial_y)
    share_q = full_dot(share_y, lower_inverse(gram_total), 1, 1)
    basis_out = (basis_scale * share_q).astype(jnp.bfloat16)
    q_round = lax.all_gather(share_q.astype(jnp.bfloat16), "cols", axis=0, tiled=True)
    partial_p = lax.dot_general(
        q_round, matrix, (((0,), (1,)), ((), ())), preferred_element_type=jnp.float32
    ).reshape(samples, wall_cells)
    projected = project_scatter(partial_p.astype(jnp.bfloat16))
    return (basis_out, projected)


def solution(mesh):
    placed = (
        P(None, "rows"),
        P("rows"),
        P(None, "cols"),
        P("cols"),
        P("cols", None),
        P("rows", "cols", None, None),
        P("rows", "cols"),
    )
    return jax.shard_map(
        per_device,
        mesh=mesh,
        in_specs=placed,
        out_specs=(P(("rows", "cols"), None), P("rows", "cols")),
        check_vma=False,
    )
```

```python
import functools
import math

import jax
import jax.numpy as jnp
import numpy as np
from jax import lax
from jax.experimental import pallas as pl
from jax.experimental.pallas import tpu as pltpu
from jax.sharding import PartitionSpec as P

TILE = 256


WAVENUMBER = 150.0
WALL_GAP = 2.0
HIGHEST = lax.Precision.HIGHEST
CHUNK = 32
TURN_HIGH = 6.28125
TURN_LOW = float(2.0 * np.pi - 6.28125)


def half_cos_terms(degree=4):
    top = np.pi**2 * 1.0001
    series = np.polynomial.Chebyshev.interpolate(
        lambda w: np.cos(np.sqrt(np.maximum(w, 0.0)) / 2.0), degree, domain=[0.0, top]
    )
    return [float(c) for c in series.convert(kind=np.polynomial.Polynomial).coef]


def tile_values(row_part, col_part):
    diff_x = row_part[:, 0:1] - col_part[0:1, :]
    diff_y = row_part[:, 1:2] - col_part[1:2, :]
    diff_z = row_part[:, 2:3] - col_part[2:3, :] - WALL_GAP
    square = diff_x * diff_x + diff_y * diff_y + diff_z * diff_z
    inverse = lax.rsqrt(square)
    distance = square * inverse
    distance = distance + (0.5 * inverse) * (square - distance * distance)
    angle = WAVENUMBER * distance
    turns = jnp.floor(angle * float(0.5 / np.pi) + 0.5)
    rest = (angle - turns * TURN_HIGH) - turns * TURN_LOW
    w = rest * rest
    terms = half_cos_terms()
    half = jnp.full_like(w, terms[-1])
    for term in terms[-2::-1]:
        half = half * w + term
    cosine = 2.0 * (half * half) - 1.0
    return (row_part[:, 3:4] * col_part[3:4, :]) * cosine * inverse


def tiles_kernel(list_ref, count_ref, rows_ref, walls_ref, matrix_ref):
    tile = walls_ref.shape[2]
    matrix_ref[...] = jnp.zeros_like(matrix_ref)

    def slot(index, carry):
        row_block = list_ref[index, 0]
        col_block = list_ref[index, 1]
        col_part = walls_ref[col_block]

        def chunk(step, inner):
            start = pl.multiple_of(row_block * tile + step * CHUNK, CHUNK)
            values = tile_values(rows_ref[pl.ds(start, CHUNK), :], col_part)
            matrix_ref[col_block, pl.ds(start, CHUNK), :] = values.astype(jnp.bfloat16)
            return inner

        return lax.fori_loop(0, tile // CHUNK, chunk, carry, unroll=2)

    lax.fori_loop(0, count_ref[0], slot, 0)


def dense_tiles(capsule_points, capsule_weight, wall_points, wall_weight, local_list, count):
    local_rows = capsule_points.shape[1]
    col_blocks = wall_points.shape[1] // TILE
    rows = jnp.concatenate([capsule_points, capsule_weight[None]], axis=0).T
    walls = jnp.concatenate([wall_points, wall_weight[None]], axis=0)
    walls = walls.reshape(4, col_blocks, TILE).transpose(1, 0, 2)
    smem = pl.BlockSpec(memory_space=pltpu.SMEM)
    vmem = pl.BlockSpec(memory_space=pltpu.VMEM)
    return pl.pallas_call(
        tiles_kernel,
        out_shape=jax.ShapeDtypeStruct((col_blocks, local_rows, TILE), jnp.bfloat16),
        in_specs=[smem, smem, vmem, vmem],
        out_specs=vmem,
        compiler_params=pltpu.CompilerParams(vmem_limit_bytes=40 * 2**20),
    )(local_list, count, rows, walls)


PANEL = 8
BLOCK = 128


def full_dot(left, right, left_dim, right_dim):
    return lax.dot_general(
        left,
        right,
        (((left_dim,), (right_dim,)), ((), ())),
        precision=HIGHEST,
        preferred_element_type=jnp.float32,
    )


def eliminate_panel(panel, first):
    lanes = lax.broadcasted_iota(jnp.int32, (PANEL, BLOCK), 1)
    subs = lax.broadcasted_iota(jnp.int32, (PANEL, BLOCK), 0)
    left = panel[:, :BLOCK]
    right = panel[:, BLOCK:]
    columns = [
        jnp.broadcast_to(
            jnp.sum(jnp.where(lanes == first + j, left, 0.0), axis=1, keepdims=True),
            (PANEL, BLOCK),
        )
        for j in range(PANEL)
    ]
    for j in range(PANEL):
        pivot = jnp.broadcast_to(columns[j][j : j + 1, :], (PANEL, BLOCK))
        scale = lax.rsqrt(pivot)
        scale = scale * (1.5 - 0.5 * pivot * (scale * scale))
        multiplier = columns[j] * scale

        def step(value):
            row = jnp.broadcast_to(value[j : j + 1, :], (PANEL, BLOCK)) * scale
            return jnp.where(subs == j, row, jnp.where(subs > j, value - multiplier * row, value))

        left = step(left)
        right = step(right)
        for k in range(j + 1, PANEL):
            columns[k] = step(columns[k])
    return left, right


def inverse_kernel(gram_ref, inverse_ref, work, small):
    size = gram_ref.shape[0]
    lanes = lax.broadcasted_iota(jnp.int32, (PANEL, BLOCK), 1)
    rows_eye = lax.broadcasted_iota(jnp.int32, (BLOCK, BLOCK), 0)
    cols_eye = lax.broadcasted_iota(jnp.int32, (BLOCK, BLOCK), 1)
    eye = jnp.where(rows_eye == cols_eye, 1.0, 0.0).astype(jnp.float32)
    work[:, :size] = gram_ref[...]
    work[:, size:] = jnp.zeros((size, size), jnp.float32)
    inverse_ref[...] = jnp.zeros_like(inverse_ref)
    for start in range(0, size, BLOCK):
        stop = start + BLOCK
        small[:, :BLOCK] = work[start:stop, start:stop]
        small[:, BLOCK:] = eye

        def group(index, carry):
            first = pl.multiple_of(index * PANEL, PANEL)
            left, right = eliminate_panel(small[pl.ds(first, PANEL), :], first)
            both = jnp.concatenate([left, right], axis=1)
            below = jnp.where(lanes >= first + PANEL, left, 0.0)
            small[...] = small[...] - full_dot(below, both, 0, 0)
            small[pl.ds(first, PANEL), :] = both
            return carry

        lax.fori_loop(0, BLOCK // PANEL, group, 0)
        block_inverse = small[:, BLOCK:]
        if start:
            known = full_dot(block_inverse, work[start:stop, size : size + start], 1, 0)
            inverse_ref[start:stop, :start] = known
        inverse_ref[start:stop, start:stop] = block_inverse
        if stop < size:
            ahead = full_dot(block_inverse, work[start:stop, stop:size], 1, 0)
            done = inverse_ref[start:stop, :stop]
            work[stop:, stop:size] = work[stop:, stop:size] - full_dot(ahead, ahead, 0, 0)
            work[stop:, size : size + stop] = work[stop:, size : size + stop] - full_dot(
                ahead, done, 0, 0
            )


def lower_inverse(gram_total):
    size = gram_total.shape[0]
    vmem = pl.BlockSpec(memory_space=pltpu.VMEM)
    return pl.pallas_call(
        inverse_kernel,
        out_shape=jax.ShapeDtypeStruct((size, size), jnp.float32),
        in_specs=[vmem],
        out_specs=vmem,
        scratch_shapes=[
            pltpu.VMEM((size, 2 * size), jnp.float32),
            pltpu.VMEM((BLOCK, 2 * BLOCK), jnp.float32),
        ],
        compiler_params=pltpu.CompilerParams(vmem_limit_bytes=32 * 2**20),
    )(gram_total)


def greet(peers):
    barrier = pltpu.get_barrier_semaphore()
    for peer in peers:
        pl.semaphore_signal(
            barrier, inc=1, device_id=peer, device_id_type=pl.DeviceIdType.MESH
        )
    pl.semaphore_wait(barrier, len(peers))


def send(source, target, send_sem, recv_sem, peer):
    copy = pltpu.make_async_remote_copy(
        src_ref=source,
        dst_ref=target,
        send_sem=send_sem,
        recv_sem=recv_sem,
        device_id=peer,
        device_id_type=pl.DeviceIdType.MESH,
    )
    copy.start()
    return copy


def wait_all(copies):
    for copy in copies:
        copy.wait()


def toggled(index, mask):
    bit = 1
    while bit <= mask:
        if mask & bit:
            index = index + bit * (1 - 2 * ((index // bit) % 2))
        bit *= 2
    return index


def tree_gather(n_cols, shares, send_sem, recv_sem, use):
    me_row = lax.axis_index("rows")
    me_col = lax.axis_index("cols")
    copies = {}
    for mask in range(n_cols):
        if mask:
            copies[mask].wait()
        slot = toggled(me_col, mask)
        bit = 1
        while bit < (mask & -mask if mask else n_cols):
            copies[mask | bit] = send(
                shares.at[slot],
                shares.at[slot],
                send_sem.at[(mask | bit) - 1],
                recv_sem.at[(mask | bit) - 1],
                (me_row, toggled(me_col, bit)),
            )
            bit *= 2
        use(mask, slot)


def sketch_kernel(
    n_rows,
    n_cols,
    y_ref,
    share_ref,
    gram_ref,
    totals,
    first_in,
    later_out,
    later_in,
    gram_own,
    col_in,
    row_sum,
    row_in,
    whole,
    first_send,
    first_recv,
    later_send,
    later_recv,
    col_send,
    col_recv,
    row_send,
    row_recv,
):
    me_row = lax.axis_index("rows")
    me_col = lax.axis_index("cols")
    row_peers = [
        (lax.rem(me_row + d, n_rows), me_col) for d in range(1, n_rows)
    ]
    col_peers = [
        (me_row, lax.rem(me_col + d, n_cols)) for d in range(1, n_cols)
    ]
    greet(row_peers + col_peers)

    half = n_cols // 2
    bit = me_col % 2
    other = (me_row, me_col + 1 - 2 * bit)
    copies = [
        send(y_ref.at[1 - bit + 2 * j], first_in.at[j], first_send.at[j], first_recv.at[j], other)
        for j in range(half)
    ]
    for j in range(half):
        copies[j].wait()
        totals[j] = y_ref[bit + 2 * j] + first_in[j]
    stride, slot = 1, 0
    while stride < half:
        low = (me_col // 2) % stride
        bit = (me_col // (2 * stride)) % 2
        other = (me_row, me_col + 2 * stride * (1 - 2 * bit))
        copies = []
        base = slot
        for j in range(half // (2 * stride)):
            source = low + stride * (1 - bit) + 2 * stride * j
            later_out[slot] = totals[source].astype(jnp.bfloat16)
            copies.append(
                send(
                    later_out.at[slot],
                    later_in.at[slot],
                    later_send.at[slot],
                    later_recv.at[slot],
                    other,
                )
            )
            slot += 1
        for j, copy in enumerate(copies):
            copy.wait()
            kept = low + stride * bit + 2 * stride * j
            totals[kept] = totals[kept] + later_in[base + j].astype(jnp.float32)
        stride *= 2
    share = totals[me_col // 2]
    share_ref[...] = share

    gram = full_dot(share, share, 0, 0)
    gram_own[...] = gram.reshape(gram_own.shape)
    copies = [
        send(gram_own.at[peer[1]], col_in.at[d], col_send.at[0, d], col_recv.at[0, d], peer)
        for d, peer in enumerate(col_peers)
    ]
    wait_all(copies)
    total = gram_own[me_col]
    for d in range(n_cols - 1):
        total = total + col_in[d]
    row_sum[...] = total
    copies = [
        send(row_sum.at[peer[0]], row_in.at[d], row_send.at[0, d], row_recv.at[0, d], peer)
        for d, peer in enumerate(row_peers)
    ]
    wait_all(copies)
    total = row_sum[me_row]
    for d in range(n_rows - 1):
        total = total + row_in[d]
    whole[me_col, me_row] = total
    mine = whole.at[me_col, me_row]
    copies = [
        send(mine, mine, row_send.at[1, d], row_recv.at[1, d], peer)
        for d, peer in enumerate(row_peers)
    ]
    wait_all(copies)
    tree_gather(n_cols, whole, col_send.at[1], col_recv.at[1], lambda mask, slot: None)
    gram_ref[...] = whole[...]


def sketch_and_gram(partial_y):
    n_rows, n_cols = lax.axis_size("rows"), lax.axis_size("cols")
    local_rows, samples = partial_y.shape
    share = local_rows // n_cols
    half = n_cols // 2
    part = samples // (n_rows * n_cols)
    vmem = pl.BlockSpec(memory_space=pltpu.VMEM)
    later = max(half - 1, 1)
    dma = pltpu.SemaphoreType.DMA
    share_y, gram = pl.pallas_call(
        functools.partial(sketch_kernel, n_rows, n_cols),
        out_shape=(
            jax.ShapeDtypeStruct((share, samples), jnp.float32),
            jax.ShapeDtypeStruct((n_cols, n_rows, part, samples), jnp.float32),
        ),
        in_specs=[vmem],
        out_specs=(vmem, vmem),
        scratch_shapes=[
            pltpu.VMEM((half, share, samples), jnp.float32),
            pltpu.VMEM((half, share, samples), jnp.float32),
            pltpu.VMEM((later, share, samples), jnp.bfloat16),
            pltpu.VMEM((later, share, samples), jnp.bfloat16),
            pltpu.VMEM((n_cols, n_rows, part, samples), jnp.float32),
            pltpu.VMEM((n_cols - 1, n_rows, part, samples), jnp.float32),
            pltpu.VMEM((n_rows, part, samples), jnp.float32),
            pltpu.VMEM((n_rows - 1, part, samples), jnp.float32),
            pltpu.VMEM((n_cols, n_rows, part, samples), jnp.float32),
            dma((half,)),
            dma((half,)),
            dma((later,)),
            dma((later,)),
            dma((2, n_cols - 1)),
            dma((2, n_cols - 1)),
            dma((2, n_rows - 1)),
            dma((2, n_rows - 1)),
        ],
        compiler_params=pltpu.CompilerParams(
            collective_id=0, has_side_effects=True, vmem_limit_bytes=48 * 2**20
        ),
    )(partial_y.reshape(n_cols, share, samples))
    return share_y, gram.reshape(samples, samples)


def finish_kernel(
    n_rows,
    n_cols,
    basis_scale,
    share_ref,
    inverse_ref,
    matrix_ref,
    basis_ref,
    out_ref,
    matrix,
    shares,
    total,
    leaving,
    arrived,
    load_sem,
    gather_send,
    gather_recv,
    send_sem,
    recv_sem,
):
    me_row = lax.axis_index("rows")
    me_col = lax.axis_index("cols")
    row_peers = [(lax.rem(me_row + d, n_rows), me_col) for d in range(1, n_rows)]
    col_peers = [(me_row, lax.rem(me_col + d, n_cols)) for d in range(1, n_cols)]
    load = pltpu.make_async_copy(matrix_ref, matrix, load_sem)
    load.start()
    greet(row_peers + col_peers)
    share_rows = share_ref.shape[0]
    col_blocks, _, tile = matrix.shape
    groups, _, part, width = leaving.shape
    share_q = full_dot(share_ref[...], inverse_ref[...], 1, 1)
    shares[me_col] = share_q.T.astype(jnp.bfloat16)
    basis_ref[...] = (basis_scale * share_q).astype(jnp.bfloat16)
    copies = []

    def product(slot, block):
        rows = pl.ds(pl.multiple_of(slot * share_rows, share_rows), share_rows)
        return jnp.dot(
            shares[slot], matrix[block, rows, :], preferred_element_type=jnp.float32
        )

    def use(mask, slot):
        if mask == 0:
            load.wait()
        for block in range(col_blocks):
            value = product(slot, block)
            if mask:
                value = value + total[block]
            if mask < n_cols - 1:
                total[block] = value
                continue
            group, place = divmod(block * tile, width)
            leaving[group, :, :, place : place + tile] = value.reshape(
                n_rows, part, tile
            ).astype(jnp.bfloat16)
            if place + tile == width:
                for d, peer in enumerate(row_peers):
                    copies.append(
                        send(
                            leaving.at[group, peer[0]],
                            arrived.at[d, group],
                            send_sem.at[d, group],
                            recv_sem.at[d, group],
                            peer,
                        )
                    )

    tree_gather(n_cols, shares, gather_send, gather_recv, use)
    wait_all(copies)
    for group in range(groups):
        value = leaving[group, me_row].astype(jnp.float32)
        for d in range(n_rows - 1):
            value = value + arrived[d, group].astype(jnp.float32)
        out_ref[:, group * width : (group + 1) * width] = value


def finish(share_y, inverse, matrix, basis_scale):
    n_rows, n_cols = lax.axis_size("rows"), lax.axis_size("cols")
    share_rows, samples = share_y.shape
    col_blocks, local_rows, tile = matrix.shape
    wall_cells = col_blocks * tile
    part = samples // n_rows
    groups = 2
    width = wall_cells // groups
    vmem = pl.BlockSpec(memory_space=pltpu.VMEM)
    dma = pltpu.SemaphoreType.DMA
    return pl.pallas_call(
        functools.partial(finish_kernel, n_rows, n_cols, basis_scale),
        out_shape=(
            jax.ShapeDtypeStruct((share_rows, samples), jnp.bfloat16),
            jax.ShapeDtypeStruct((part, wall_cells), jnp.float32),
        ),
        in_specs=[vmem, vmem, pl.BlockSpec(memory_space=pl.ANY)],
        out_specs=(vmem, vmem),
        scratch_shapes=[
            pltpu.VMEM(matrix.shape, jnp.bfloat16),
            pltpu.VMEM((n_cols, samples, share_rows), jnp.bfloat16),
            pltpu.VMEM((col_blocks, samples, tile), jnp.float32),
            pltpu.VMEM((groups, n_rows, part, width), jnp.bfloat16),
            pltpu.VMEM((n_rows - 1, groups, part, width), jnp.bfloat16),
            dma,
            dma((n_cols - 1,)),
            dma((n_cols - 1,)),
            dma((n_rows - 1, groups)),
            dma((n_rows - 1, groups)),
        ],
        compiler_params=pltpu.CompilerParams(
            collective_id=1, has_side_effects=True, vmem_limit_bytes=48 * 2**20
        ),
    )(share_y, inverse, matrix)


def per_device(
    capsule_points, capsule_weight, wall_points, wall_weight, gauss_sketch, far_pairs, tile_count
):
    row_dev = lax.axis_index("rows")
    col_dev = lax.axis_index("cols")
    local_rows = capsule_points.shape[1]
    wall_cells = wall_points.shape[1]
    row_blocks = local_rows // TILE
    col_blocks = wall_cells // TILE
    samples = gauss_sketch.shape[1]
    offset = jnp.stack([row_dev * row_blocks, col_dev * col_blocks]).astype(jnp.int32)
    matrix = dense_tiles(
        capsule_points,
        capsule_weight,
        wall_points,
        wall_weight,
        far_pairs[0, 0] - offset[None, :],
        tile_count[0],
    )
    partial_y = lax.dot_general(
        matrix,
        gauss_sketch.reshape(col_blocks, TILE, samples),
        (((0, 2), (0, 1)), ((), ())),
        preferred_element_type=jnp.float32,
    )
    basis_scale = math.sqrt(local_rows * lax.axis_size("rows"))
    share_y, gram_total = sketch_and_gram(partial_y)
    return finish(share_y, lower_inverse(gram_total), matrix, basis_scale)


def solution(mesh):
    placed = (
        P(None, "rows"),
        P("rows"),
        P(None, "cols"),
        P("cols"),
        P("cols", None),
        P("rows", "cols", None, None),
        P("rows", "cols"),
    )
    return jax.shard_map(
        per_device,
        mesh=mesh,
        in_specs=placed,
        out_specs=(P(("rows", "cols"), None), P("rows", "cols")),
        check_vma=False,
    )
```
